256 devices in a mesh: patch: 16 (over z_lo, x), head: 16 (over z_hi, y, core).
Axes of the slice: x: 4, y: 4, z: 8 (z_hi: 2, z_lo: 4; z = z_hi * 4 + z_lo), core: 2. Of those that a mesh axis runs over, the one named last changes fastest.
Arguments:
- queries: bfloat16 [2048, 6144], P('patch', 'head'), may hold values from -17 to 17
- stale_kv: float32 [2, 2048, 6144], P(None, None, 'head'), may hold values from -8 to 8, as said below
- delta_kv: bfloat16 [2, 2048, 6144], P(None, 'patch', 'head'), may hold values from -17 to 17
- out_weight: bfloat16 [6144, 6144], P('head'), may hold values from -0.078125 to 0.078125
Outputs:
- projected: bfloat16 [2048, 6144], P(('patch', 'head'))
The draws below stay inside these ranges and needn't reach their ends.
Inputs may be any that keep to these rules, and one draw needn't show every extreme that they name: `stale_kv`: stored keys and values of order one.
All inputs are finite; a program needn't handle non-finite values.
Results may differ from the reference program's by a relative error of at most 0.019.
Values may be sent and summed in bfloat16 or wider, within the bound.
A program may use at most 64 MiB of HBM per device.

```python
import math
import jax
import jax.numpy as jnp
from jax import lax

D = 6144
HEADS = 48
HD = 128
TOKENS = 2048


def spread_field(key, shape, scale):
    return scale * jnp.clip(jax.random.normal(key, shape, jnp.float32), -4.0, 4.0)


def draw_queries(key, part):
    key = jax.random.fold_in(key, 11)
    values = spread_field(key, (TOKENS, HEADS * HD), 1.5)
    return values.astype(jnp.bfloat16)


def draw_stale_kv(key, part):
    key = jax.random.fold_in(key, 13)
    first, second = jax.random.split(key)
    stored_keys = spread_field(first, (TOKENS, HEADS * HD), 1.0)
    stored_values = spread_field(second, (TOKENS, HEADS * HD), 2.0)
    return jnp.stack([stored_keys, stored_values]).astype(jnp.float32)


def draw_delta_kv(key, part):
    key = jax.random.fold_in(key, 17)
    first, second = jax.random.split(key)
    change_keys = spread_field(first, (TOKENS, HEADS * HD), 0.5)
    change_values = spread_field(second, (TOKENS, HEADS * HD), 2.0)
    return jnp.stack([change_keys, change_values]).astype(jnp.bfloat16)


def shard_levels(rng, extent, cuts, least, top_value):
    gain, own = 1.0, jax.random.fold_in(rng, 6)
    for axis_at, blocks in cuts:
        steps = jnp.exp(jax.random.uniform(jax.random.fold_in(own, axis_at), (blocks,), jnp.float32, least / len(cuts), top_value / len(cuts)))
        gain = gain * jnp.repeat(steps, extent[axis_at] // blocks).reshape([-1 if axis == axis_at else 1 for axis in range(len(extent))])
    return gain


def gaussian(stream_key, shape, deviation, most, cuts=(), held_as=jnp.bfloat16):
    values = deviation * jax.random.normal(stream_key, shape, jnp.float32)
    if cuts:
        values = values * shard_levels(stream_key, shape, cuts, -0.22, 0.18)
    return jnp.clip(values, -most, most).astype(held_as)


def setup_inputs(seed: int = 0) -> dict:
    keys = jax.random.split(jax.random.key(seed), 5)
    return {
        "queries": draw_queries(jax.random.fold_in(keys[4], 71), 0),
        "stale_kv": draw_stale_kv(jax.random.fold_in(keys[4], 71), 0),
        "delta_kv": draw_delta_kv(jax.random.fold_in(keys[4], 71), 0),
        "out_weight": gaussian(keys[3], (HEADS * HD, D), (HEADS * HD) ** -0.5, 0.078125, ((0, 16),)),
    }


def one_head(operands):
    query_head, key_head, value_head = operands
    scores = jnp.dot(query_head, key_head.T, preferred_element_type=jnp.float32) * (1.0 / math.sqrt(HD))
    peak = lax.optimization_barrier(jnp.max(scores, axis=1, keepdims=True))
    expo = jnp.exp(scores - peak)
    weights = expo.astype(jnp.bfloat16)
    denom = lax.optimization_barrier(jnp.sum(expo, axis=1, keepdims=True))
    mixed = jnp.dot(weights, value_head, preferred_element_type=jnp.float32)
    return (mixed / denom).astype(jnp.bfloat16)

def heads_first(tensor):
    return jnp.transpose(tensor.reshape(TOKENS, HEADS, HD), (1, 0, 2))

def reference(queries, stale_kv, delta_kv, out_weight):
    refreshed = (stale_kv + delta_kv.astype(jnp.float32)).astype(jnp.bfloat16)
    attended = lax.map(one_head, (heads_first(queries), heads_first(refreshed[0]), heads_first(refreshed[1])))
    attended = jnp.transpose(attended, (1, 0, 2)).reshape(TOKENS, HEADS * HD)
    return jnp.dot(attended, out_weight, preferred_element_type=jnp.float32).astype(jnp.bfloat16)
```

```python
import functools
import math

import jax
import jax.numpy as jnp
from jax import lax
from jax.experimental import pallas as pl
from jax.experimental.pallas import tpu as pltpu
from jax.sharding import PartitionSpec as P

MESH = pl.DeviceIdType.MESH
F32, BF16 = jnp.float32, jnp.bfloat16

HD = 128
HEADS = 3
TOK = 128
RING = 4
COLS = HEADS * HD
D = 6144
CHUNKS = 6
WIDTH = D // CHUNKS
PART = HD + 16
SCALE = 1.0 / math.sqrt(HD)


def split3(value):
    high = value.astype(BF16).astype(F32)
    rest = value - high
    middle = rest.astype(BF16).astype(F32)
    return high, middle, rest - middle


def kernel(
    q_ref, stale_ref, delta_ref, w_ref, out_ref,
    stale_v, kv, qs, part_out, part_in, w_v, att, own, sib_out, sib_in, y_out, y_in, z_own, z_out, z_in,
    local_sem, kv_s, kv_r, q_s, q_r, o_s, o_r, sib_s, sib_r, y_s, y_r, z_s, z_r,
):
    patch, head = lax.axis_index("patch"), lax.axis_index("head")
    z, x = patch // RING, lax.rem(patch, RING)
    z_hi, y, core = head // 8, lax.rem(head // 2, RING), lax.rem(head, 2)

    def at_x(k):
        return (z * RING + lax.rem(x + k + RING, RING), head)

    def at_z(k):
        return (lax.rem(z + k + RING, RING) * RING + x, head)

    def at_y(k):
        return (patch, z_hi * 8 + lax.rem(y + k, RING) * 2 + core)

    sibling = (patch, z_hi * 8 + y * 2 + (1 - core))
    across = (patch, (1 - z_hi) * 8 + y * 2 + core)

    def remote(src, dst, send, recv, device):
        return pltpu.make_async_remote_copy(
            src_ref=src, dst_ref=dst, send_sem=send, recv_sem=recv, device_id=device, device_id_type=MESH
        )

    local = []
    for k in range(RING):
        row = (z * RING + lax.rem(x - k + RING, RING)) * TOK
        local.append(pltpu.make_async_copy(stale_ref.at[:, pl.ds(row, TOK), :], stale_v.at[k], local_sem.at[k]))
    for h in range(HEADS):
        cols = pl.ds(h * HD, HD)
        local.append(pltpu.make_async_copy(delta_ref.at[:, :, cols], kv.at[h, 0], local_sem.at[4 + h]))
        local.append(pltpu.make_async_copy(q_ref.at[:, cols], qs.at[h, 0], local_sem.at[7 + h]))
    weight = pltpu.make_async_copy(w_ref, w_v, local_sem.at[10])
    for copy in local:
        copy.start()
    weight.start()

    barrier = pltpu.get_barrier_semaphore()
    partners = [at_x(k) for k in (1, 2, 3)] + [at_z(k) for k in (1, 2, 3)] + [at_y(k) for k in (1, 2, 3)] + [sibling, across]
    for device in partners:
        pl.semaphore_signal(barrier, inc=1, device_id=device, device_id_type=MESH)
    pl.semaphore_wait(barrier, len(partners))

    kv_copies, q_copies = {}, {}
    for h in range(HEADS):
        cols = pl.ds(h * HD, HD)
        for k in (1, 2, 3):
            kv_copies[h, k] = remote(
                delta_ref.at[:, :, cols], kv.at[h, k], kv_s.at[h, k - 1], kv_r.at[h, k - 1], at_x(k)
            )
            q_copies[h, k] = remote(q_ref.at[:, cols], qs.at[h, k], q_s.at[h, k - 1], q_r.at[h, k - 1], at_z(k))
        for k in (1, 2, 3):
            kv_copies[h, k].start()
            q_copies[h, k].start()

    for copy in local:
        copy.wait()

    o_copies = {}
    for h in range(HEADS):
        cols = slice(h * HD, (h + 1) * HD)
        keys, values = [], []
        for k in range(RING):
            if k:
                kv_copies[h, k].wait_recv()
            fresh = stale_v[k, :, :, cols] + kv[h, k].astype(F32)
            keys.append(fresh[0].astype(BF16))
            values.append(fresh[1].T.astype(BF16))
        keys = jnp.concatenate(keys, axis=0)
        values = jnp.concatenate(values, axis=1)
        for k in (1, 2, 3, 0):
            if k:
                q_copies[h, k].wait_recv()
            scores = lax.dot_general(keys, qs[h, k], (((1,), (1,)), ((), ())), preferred_element_type=F32)
            peak = jnp.max(scores, axis=0, keepdims=True)
            expo = jnp.exp((scores - peak) * SCALE)
            denom = jnp.sum(expo, axis=0, keepdims=True)
            mixed = jnp.dot(values, expo.astype(BF16), preferred_element_type=F32) / denom
            row = lax.broadcasted_iota(jnp.int32, (16, TOK), 0)
            stats = jnp.zeros((16, TOK), F32)
            for i, term in enumerate(split3(peak * SCALE) + split3(denom)):
                stats = jnp.where(row == i, term, stats)
            buffer = part_out if k else part_in
            buffer[h, k, :HD, :] = mixed.astype(BF16)
            buffer[h, k, HD:, :] = stats.astype(BF16)
            if k:
                o_copies[h, k] = remote(
                    part_out.at[h, k], part_in.at[h, k], o_s.at[h, k - 1], o_r.at[h, k - 1], at_z(RING - k)
                )
                o_copies[h, k].start()

    for h in range(HEADS):
        peaks, denoms = [], []
        for k in range(RING):
            if k:
                o_copies[h, k].wait_recv()
            stats = part_in[h, k, HD:, :].astype(F32)
            peaks.append(stats[0:1] + stats[1:2] + stats[2:3])
            denoms.append(stats[3:4] + stats[4:5] + stats[5:6])
        top = functools.reduce(jnp.maximum, peaks)
        shares = [d * jnp.exp(p - top) for p, d in zip(peaks, denoms)]
        total = functools.reduce(jnp.add, shares)
        merged = functools.reduce(
            jnp.add, [part_in[h, k, :HD, :].astype(F32) * (shares[k] / total) for k in range(RING)]
        ).T
        by_core = [
            jnp.concatenate(
                [merged[(zz * 8 + yy * 2 + c) * 8 :][:8] for yy in range(RING) for zz in range(2)], axis=0
            )
            for c in range(2)
        ]
        mine = jnp.where(core == 0, by_core[0], by_core[1])
        other = jnp.where(core == 0, by_core[1], by_core[0])
        att[0:64, h * HD : (h + 1) * HD] = mine.astype(BF16)
        att[64:128, h * HD : (h + 1) * HD] = other.astype(BF16)

    weight.wait()
    sib_copies, y_copies, z_copies = {}, {}, {}

    def project(j):
        cols = slice(j * WIDTH, (j + 1) * WIDTH)
        prod = jnp.dot(att[...], w_v[:, cols], preferred_element_type=F32)
        own[:, :, cols] = prod[:64].reshape(RING, 16, WIDTH)
        sib_out[j] = prod[64:].astype(BF16)
        sib_copies[j] = remote(sib_out.at[j], sib_in.at[j], sib_s.at[j], sib_r.at[j], sibling)
        sib_copies[j].start()

    def to_y(j):
        cols = slice(j * WIDTH, (j + 1) * WIDTH)
        sib_copies[j].wait_recv()
        pair = own[:, :, cols] + sib_in[j].astype(F32).reshape(RING, 16, WIDTH)
        own[:, :, cols] = pair
        y_out[j] = pair.astype(BF16)
        for k in (1, 2, 3):
            y_copies[j, k] = remote(
                y_out.at[j, lax.rem(y + k, RING)], y_in.at[j, k - 1], y_s.at[j, k - 1], y_r.at[j, k - 1], at_y(k)
            )
            y_copies[j, k].start()

    def to_z(j):
        cols = slice(j * WIDTH, (j + 1) * WIDTH)
        total = own[y, :, cols]
        for k in (1, 2, 3):
            y_copies[j, k].wait_recv()
            total = total + y_in[j, k - 1].astype(F32)
        z_own[0, :, cols] = total[:8]
        z_own[1, :, cols] = total[8:]
        half = WIDTH // 2
        away = z_own[1 - z_hi, :, cols]
        z_out[j] = jnp.concatenate([away[:, :half], away[:, half:]], axis=0).astype(BF16)
        z_copies[j] = remote(z_out.at[j], z_in.at[j], z_s.at[j], z_r.at[j], across)
        z_copies[j].start()

    def finish(j):
        z_copies[j].wait_recv()
        half = WIDTH // 2
        for i in range(2):
            cols = slice(j * WIDTH + i * half, j * WIDTH + (i + 1) * half)
            came = z_in[j].astype(F32)[i * 8 : (i + 1) * 8]
            out_ref[:, cols] = (z_own[z_hi, :, cols] + came).astype(BF16)

    stages = (project, to_y, to_z, finish)
    lags = (0, 2, 6, 8)
    for t in range(CHUNKS + lags[-1]):
        for stage, lag in zip(stages, lags):
            if 0 <= t - lag < CHUNKS:
                stage(t - lag)

    for copies in (kv_copies, q_copies, o_copies, sib_copies, y_copies, z_copies):
        for copy in copies.values():
            copy.wait_send()


def body(queries, stale_kv, delta_kv, out_weight):
    dma = pltpu.SemaphoreType.DMA
    return pl.pallas_call(
        kernel,
        name="sublayer",
        out_shape=jax.ShapeDtypeStruct((8, D), BF16),
        in_specs=[pl.BlockSpec(memory_space=pl.ANY)] * 4,
        out_specs=pl.BlockSpec(memory_space=pltpu.VMEM),
        scratch_shapes=[
            pltpu.VMEM((RING, 2, TOK, COLS), F32),
            pltpu.VMEM((HEADS, RING, 2, TOK, HD), BF16),
            pltpu.VMEM((HEADS, RING, TOK, HD), BF16),
            pltpu.VMEM((HEADS, RING, PART, TOK), BF16),
            pltpu.VMEM((HEADS, RING, PART, TOK), BF16),
            pltpu.VMEM((COLS, D), BF16),
            pltpu.VMEM((TOK, COLS), BF16),
            pltpu.VMEM((RING, 16, D), F32),
            pltpu.VMEM((CHUNKS, 64, WIDTH), BF16),
            pltpu.VMEM((CHUNKS, 64, WIDTH), BF16),
            pltpu.VMEM((CHUNKS, RING, 16, WIDTH), BF16),
            pltpu.VMEM((CHUNKS, RING - 1, 16, WIDTH), BF16),
            pltpu.VMEM((2, 8, D), F32),
            pltpu.VMEM((CHUNKS, 16, WIDTH // 2), BF16),
            pltpu.VMEM((CHUNKS, 16, WIDTH // 2), BF16),
            dma((11,)),
            dma((HEADS, 3)),
            dma((HEADS, 3)),
            dma((HEADS, 3)),
            dma((HEADS, 3)),
            dma((HEADS, 3)),
            dma((HEADS, 3)),
            dma((CHUNKS,)),
            dma((CHUNKS,)),
            dma((CHUNKS, 3)),
            dma((CHUNKS, 3)),
            dma((CHUNKS,)),
            dma((CHUNKS,)),
        ],
        compiler_params=pltpu.CompilerParams(
            collective_id=0, has_side_effects=True, vmem_limit_bytes=60 * 1024 * 1024
        ),
    )(queries, stale_kv, delta_kv, out_weight)


def solution(mesh):
    return jax.shard_map(
        body,
        mesh=mesh,
        in_specs=(
            P("patch", "head"),
            P(None, None, "head"),
            P(None, "patch", "head"),
            P("head", None),
        ),
        out_specs=P(("patch", "head"), None),
        check_vma=False,
    )
```

```python
import functools
import math

import jax
import jax.numpy as jnp
from jax import lax
from jax.experimental import pallas as pl
from jax.experimental.pallas import tpu as pltpu
from jax.sharding import PartitionSpec as P

MESH = pl.DeviceIdType.MESH
F32, BF16 = jnp.float32, jnp.bfloat16

HD = 128
HEADS = 3
TOK = 128
RING = 4
COLS = HEADS * HD
D = 6144
CHUNKS = 4
WIDTH = D // CHUNKS
HALF = WIDTH // 2
PART = HD + 16
SCALE = 1.0 / math.sqrt(HD)


def split3(value):
    high = value.astype(BF16).astype(F32)
    rest = value - high
    middle = rest.astype(BF16).astype(F32)
    return high, middle, rest - middle


def kernel(
    q_ref, stale_ref, delta_ref, w_ref, out_ref,
    stale_v, kv, qs, part_out, part_in, w_v, att, own, sib_out, sib_in, y_out, y_in, y_sum, z_own, z_out, z_in,
    local_sem, kv_s, kv_r, q_s, q_r, o_s, o_r, sib_s, sib_r, y_s, y_r, z_s, z_r,
):
    patch, head = lax.axis_index("patch"), lax.axis_index("head")
    z, x = patch // RING, lax.rem(patch, RING)
    z_hi, y, core = head // 8, lax.rem(head // 2, RING), lax.rem(head, 2)

    def at_x(k):
        return (z * RING + lax.rem(x + k + RING, RING), head)

    def at_z(place):
        return (place * RING + x, head)

    def at_y(k):
        return (patch, z_hi * 8 + lax.rem(y + k + RING, RING) * 2 + core)

    others = {1: z + 1 - 2 * lax.rem(z, 2), 2: lax.rem(z + 2, RING), 3: 3 - z}
    sibling = (patch, z_hi * 8 + y * 2 + (1 - core))
    across = (patch, (1 - z_hi) * 8 + y * 2 + core)

    def remote(src, dst, send, recv, device):
        return pltpu.make_async_remote_copy(
            src_ref=src, dst_ref=dst, send_sem=send, recv_sem=recv, device_id=device, device_id_type=MESH
        )

    local = []
    for k in range(RING):
        row = (z * RING + lax.rem(x - k + RING, RING)) * TOK
        local.append(pltpu.make_async_copy(stale_ref.at[:, pl.ds(row, TOK), :], stale_v.at[k], local_sem.at[k]))
    for h in range(HEADS):
        cols = pl.ds(h * HD, HD)
        local.append(pltpu.make_async_copy(delta_ref.at[:, :, cols], kv.at[h, 0], local_sem.at[4 + h]))
        local.append(pltpu.make_async_copy(q_ref.at[:, cols], qs.at[h, 0], local_sem.at[7 + h]))
    weight = pltpu.make_async_copy(w_ref, w_v, local_sem.at[10])
    for copy in local:
        copy.start()
    weight.start()

    barrier = pltpu.get_barrier_semaphore()
    partners = [at_x(1), at_x(-1), at_y(1), at_y(-1)] + [at_z(others[k]) for k in (1, 2, 3)] + [sibling, across]
    for device in partners:
        pl.semaphore_signal(barrier, inc=1, device_id=device, device_id_type=MESH)
    pl.semaphore_wait(barrier, len(partners))

    kv_copies, q_copies = {}, {}
    for h in range(HEADS):
        cols = pl.ds(h * HD, HD)
        mine, query = delta_ref.at[:, :, cols], q_ref.at[:, cols]
        kv_copies[h, 1] = remote(mine, kv.at[h, 1], kv_s.at[h, 0], kv_r.at[h, 0], at_x(1))
        kv_copies[h, 3] = remote(mine, kv.at[h, 3], kv_s.at[h, 1], kv_r.at[h, 1], at_x(-1))
        for k in (2, 1):
            q_copies[h, k] = remote(query, qs.at[h, k], q_s.at[h, k - 1], q_r.at[h, k - 1], at_z(others[k]))
        q_copies[h, 2].start()
        kv_copies[h, 1].start()
        kv_copies[h, 3].start()
        q_copies[h, 1].start()
    for h in range(HEADS):
        kv_copies[h, 1].wait_recv()
        kv_copies[h, "k"] = remote(kv.at[h, 1, 0], kv.at[h, 2, 0], kv_s.at[h, 2], kv_r.at[h, 2], at_x(1))
        kv_copies[h, "k"].start()
        kv_copies[h, 3].wait_recv()
        kv_copies[h, "v"] = remote(kv.at[h, 3, 1], kv.at[h, 2, 1], kv_s.at[h, 3], kv_r.at[h, 3], at_x(-1))
        kv_copies[h, "v"].start()
        q_copies[h, 2].wait_recv()
        q_copies[h, 3] = remote(qs.at[h, 2], qs.at[h, 3], q_s.at[h, 2], q_r.at[h, 2], at_z(others[1]))
        q_copies[h, 3].start()

    for copy in local:
        copy.wait()

    o_copies = {}
    for h in range(HEADS):
        cols = slice(h * HD, (h + 1) * HD)
        keys, values = [], []
        for k in range(RING):
            if k == 2:
                kv_copies[h, "k"].wait_recv()
                kv_copies[h, "v"].wait_recv()
            fresh = stale_v[k, :, :, cols] + kv[h, k].astype(F32)
            keys.append(fresh[0].astype(BF16))
            values.append(fresh[1].T.astype(BF16))
        keys = jnp.concatenate(keys, axis=0)
        values = jnp.concatenate(values, axis=1)
        for k in (2, 1, 3, 0):
            if k in (1, 3):
                q_copies[h, k].wait_recv()
            scores = lax.dot_general(keys, qs[h, k], (((1,), (1,)), ((), ())), preferred_element_type=F32)
            peak = jnp.max(scores, axis=0, keepdims=True)
            expo = jnp.exp((scores - peak) * SCALE)
            denom = jnp.sum(expo, axis=0, keepdims=True)
            mixed = jnp.dot(values, expo.astype(BF16), preferred_element_type=F32) / denom
            row = lax.broadcasted_iota(jnp.int32, (16, TOK), 0)
            stats = jnp.zeros((16, TOK), F32)
            for i, term in enumerate(split3(peak * SCALE) + split3(denom)):
                stats = jnp.where(row == i, term, stats)
            buffer = part_out if k else part_in
            buffer[h, k, :HD, :] = mixed.astype(BF16)
            buffer[h, k, HD:, :] = stats.astype(BF16)
            if k:
                o_copies[h, k] = remote(
                    part_out.at[h, k], part_in.at[h, k], o_s.at[h, k - 1], o_r.at[h, k - 1], at_z(others[k])
                )
                o_copies[h, k].start()

    for h in range(HEADS):
        peaks, denoms = [], []
        for k in range(RING):
            if k:
                o_copies[h, k].wait_recv()
            stats = part_in[h, k, HD:, :].astype(F32)
            peaks.append(stats[0:1] + stats[1:2] + stats[2:3])
            denoms.append(stats[3:4] + stats[4:5] + stats[5:6])
        top = functools.reduce(jnp.maximum, peaks)
        shares = [d * jnp.exp(p - top) for p, d in zip(peaks, denoms)]
        total = functools.reduce(jnp.add, shares)
        merged = functools.reduce(
            jnp.add, [part_in[h, k, :HD, :].astype(F32) * (shares[k] / total) for k in range(RING)]
        ).T
        by_core = [
            jnp.concatenate(
                [merged[(zz * 8 + yy * 2 + c) * 8 :][:8] for yy in range(RING) for zz in range(2)], axis=0
            )
            for c in range(2)
        ]
        mine = jnp.where(core == 0, by_core[0], by_core[1])
        other = jnp.where(core == 0, by_core[1], by_core[0])
        att[0:64, h * HD : (h + 1) * HD] = mine.astype(BF16)
        att[64:128, h * HD : (h + 1) * HD] = other.astype(BF16)

    weight.wait()
    sib_copies, y_copies, z_copies = {}, {}, {}

    def project(j):
        cols = slice(j * WIDTH, (j + 1) * WIDTH)
        prod = jnp.dot(att[...], w_v[:, cols], preferred_element_type=F32)
        own[:, :, cols] = prod[:64].reshape(RING, 16, WIDTH)
        sib_out[j] = prod[64:].astype(BF16)
        sib_copies[j] = remote(sib_out.at[j], sib_in.at[j], sib_s.at[j], sib_r.at[j], sibling)
        sib_copies[j].start()

    def to_y(j):
        cols = slice(j * WIDTH, (j + 1) * WIDTH)
        sib_copies[j].wait_recv()
        pair = own[:, :, cols] + sib_in[j].astype(F32).reshape(RING, 16, WIDTH)
        own[:, :, cols] = pair
        for i in range(2):
            y_out[j, i] = pair[:, :, i * HALF : (i + 1) * HALF].astype(BF16)
        opposite = lax.rem(y + 2, RING)
        for i, step in enumerate((1, -1)):
            y_copies[j, i] = remote(
                y_out.at[j, i, opposite], y_in.at[j, i], y_s.at[j, i], y_r.at[j, i], at_y(step)
            )
            y_copies[j, i].start()

    def direct_y(j):
        for i, step in enumerate((1, -1)):
            y_copies[j, 2 + i] = remote(
                y_out.at[j, 1 - i, lax.rem(y + step + RING, RING)],
                y_in.at[j, 2 + i], y_s.at[j, 2 + i], y_r.at[j, 2 + i], at_y(step),
            )
            y_copies[j, 2 + i].start()

    def relay_y(j):
        for i, step in enumerate((1, -1)):
            place = lax.rem(y + step + RING, RING)
            y_copies[j, i].wait_recv()
            start = j * WIDTH + i * HALF
            total = own[place, :, start : start + HALF] + y_in[j, i].astype(F32)
            y_sum[j, i] = total.astype(BF16)
            y_copies[j, 4 + i] = remote(
                y_sum.at[j, i], y_in.at[j, 4 + i], y_s.at[j, 4 + i], y_r.at[j, 4 + i], at_y(step)
            )
            y_copies[j, 4 + i].start()

    def to_z(j):
        for i in range(2):
            y_copies[j, 4 + i].wait_recv()
            y_copies[j, 3 - i].wait_recv()
            start = j * WIDTH + i * HALF
            total = own[y, :, start : start + HALF] + y_in[j, 4 + i].astype(F32) + y_in[j, 3 - i].astype(F32)
            z_own[0, :, start : start + HALF] = total[:8]
            z_own[1, :, start : start + HALF] = total[8:]
        away = z_own[1 - z_hi, :, j * WIDTH : (j + 1) * WIDTH]
        z_out[j] = jnp.concatenate([away[:, :HALF], away[:, HALF:]], axis=0).astype(BF16)
        z_copies[j] = remote(z_out.at[j], z_in.at[j], z_s.at[j], z_r.at[j], across)
        z_copies[j].start()

    def finish(j):
        z_copies[j].wait_recv()
        for i in range(2):
            cols = slice(j * WIDTH + i * HALF, j * WIDTH + (i + 1) * HALF)
            came = z_in[j].astype(F32)[i * 8 : (i + 1) * 8]
            out_ref[:, cols] = (z_own[z_hi, :, cols] + came).astype(BF16)

    stages = (project, to_y, direct_y, relay_y, to_z, finish)
    lags = (0, 1, 3, 4, 7, 11)
    for t in range(CHUNKS + lags[-1]):
        for stage, lag in zip(stages, lags):
            if 0 <= t - lag < CHUNKS:
                stage(t - lag)

    for copies in (kv_copies, q_copies, o_copies, sib_copies, y_copies, z_copies):
        for copy in copies.values():
            copy.wait_send()


def body(queries, stale_kv, delta_kv, out_weight):
    dma = pltpu.SemaphoreType.DMA
    return pl.pallas_call(
        kernel,
        name="sublayer",
        out_shape=pltpu.VMEM((8, D), BF16),
        in_specs=[pl.BlockSpec(memory_space=pl.ANY)] * 4,
        out_specs=pl.BlockSpec(memory_space=pltpu.VMEM),
        scratch_shapes=[
            pltpu.VMEM((RING, 2, TOK, COLS), F32),
            pltpu.VMEM((HEADS, RING, 2, TOK, HD), BF16),
            pltpu.VMEM((HEADS, RING, TOK, HD), BF16),
            pltpu.VMEM((HEADS, RING, PART, TOK), BF16),
            pltpu.VMEM((HEADS, RING, PART, TOK), BF16),
            pltpu.VMEM((COLS, D), BF16),
            pltpu.VMEM((TOK, COLS), BF16),
            pltpu.VMEM((RING, 16, D), F32),
            pltpu.VMEM((CHUNKS, 64, WIDTH), BF16),
            pltpu.VMEM((CHUNKS, 64, WIDTH), BF16),
            pltpu.VMEM((CHUNKS, 2, RING, 16, HALF), BF16),
            pltpu.VMEM((CHUNKS, 6, 16, HALF), BF16),
            pltpu.VMEM((CHUNKS, 2, 16, HALF), BF16),
            pltpu.VMEM((2, 8, D), F32),
            pltpu.VMEM((CHUNKS, 16, WIDTH // 2), BF16),
            pltpu.VMEM((CHUNKS, 16, WIDTH // 2), BF16),
            dma((11,)),
            dma((HEADS, 4)),
            dma((HEADS, 4)),
            dma((HEADS, 3)),
            dma((HEADS, 3)),
            dma((HEADS, 3)),
            dma((HEADS, 3)),
            dma((CHUNKS,)),
            dma((CHUNKS,)),
            dma((CHUNKS, 6)),
            dma((CHUNKS, 6)),
            dma((CHUNKS,)),
            dma((CHUNKS,)),
        ],
        compiler_params=pltpu.CompilerParams(
            collective_id=0, has_side_effects=True, vmem_limit_bytes=60 * 1024 * 1024
        ),
    )(*[pltpu.with_memory_space_constraint(a, pltpu.HBM) for a in (queries, stale_kv, delta_kv, out_weight)])


def solution(mesh):
    return jax.shard_map(
        body,
        mesh=mesh,
        in_specs=(
            P("patch", "head"),
            P(None, None, "head"),
            P(None, "patch", "head"),
            P("head", None),
        ),
        out_specs=P(("patch", "head"), None),
        check_vma=False,
    )
```

```python
import functools
import math

import jax
import jax.numpy as jnp
from jax import lax
from jax.experimental import pallas as pl
from jax.experimental.pallas import tpu as pltpu
from jax.sharding import PartitionSpec as P

MESH = pl.DeviceIdType.MESH
F32, BF16 = jnp.float32, jnp.bfloat16

HD = 128
HEADS = 3
TOK = 128
RING = 4
COLS = HEADS * HD
D = 6144
CHUNKS = 4
SIDE = D // 2
WIDTH = SIDE // CHUNKS
HALF = WIDTH // 2
SCALE = 1.0 / math.sqrt(HD)


def kernel(
    q_ref, stale_ref, delta_ref, w_ref, out_ref,
    stale_v, kv, qs, part_out, part_in, stat_out, stat_in, w_v, att, own, y_out, y_in, y_sum, z_own, z_out, z_in,
    local_sem, kv_s, kv_r, q_s, q_r, o_s, o_r, t_s, t_r, w_s, w_r, a_s, a_r, y_s, y_r, z_s, z_r,
):
    patch, head = lax.axis_index("patch"), lax.axis_index("head")
    z, x = patch // RING, lax.rem(patch, RING)
    z_hi, y, core = head // 8, lax.rem(head // 2, RING), lax.rem(head, 2)

    def at_x(k):
        return (z * RING + lax.rem(x + k + RING, RING), head)

    def at_z(place):
        return (place * RING + x, head)

    def at_y(k):
        return (patch, z_hi * 8 + lax.rem(y + k + RING, RING) * 2 + core)

    others = {1: z + 1 - 2 * lax.rem(z, 2), 2: lax.rem(z + 2, RING), 3: 3 - z}
    sibling = (patch, z_hi * 8 + y * 2 + (1 - core))
    across = (patch, (1 - z_hi) * 8 + y * 2 + core)
    opposite = (patch, (1 - z_hi) * 8 + y * 2 + (1 - core))

    def remote(src, dst, send, recv, device):
        return pltpu.make_async_remote_copy(
            src_ref=src, dst_ref=dst, send_sem=send, recv_sem=recv, device_id=device, device_id_type=MESH
        )

    local = []
    for k in range(RING):
        row = (z * RING + lax.rem(x - k + RING, RING)) * TOK
        local.append(pltpu.make_async_copy(stale_ref.at[:, pl.ds(row, TOK), :], stale_v.at[k], local_sem.at[k]))
    for h in range(HEADS):
        cols = pl.ds(h * HD, HD)
        local.append(pltpu.make_async_copy(delta_ref.at[:, :, cols], kv.at[h, 0], local_sem.at[4 + h]))
        local.append(pltpu.make_async_copy(q_ref.at[:, cols], qs.at[h, 0], local_sem.at[7 + h]))
    side = pl.ds(pl.multiple_of(core * SIDE, SIDE), SIDE)
    other_side = pl.ds(pl.multiple_of((1 - core) * SIDE, SIDE), SIDE)
    weight = pltpu.make_async_copy(w_ref.at[:, side], w_v.at[pl.ds(0, COLS)], local_sem.at[10])
    for copy in local:
        copy.start()
    weight.start()

    barrier = pltpu.get_barrier_semaphore()
    partners = [at_x(1), at_x(-1), at_y(1), at_y(-1)] + [at_z(others[k]) for k in (1, 2, 3)] + [sibling, across, opposite]
    for device in partners:
        pl.semaphore_signal(barrier, inc=1, device_id=device, device_id_type=MESH)
    pl.semaphore_wait(barrier, len(partners))

    kv_copies, q_copies = {}, {}
    for h in range(HEADS):
        cols = pl.ds(h * HD, HD)
        mine, query = delta_ref.at[:, :, cols], q_ref.at[:, cols]
        kv_copies[h, 1] = remote(mine, kv.at[h, 1], kv_s.at[h, 0], kv_r.at[h, 0], at_x(1))
        kv_copies[h, 3] = remote(mine, kv.at[h, 3], kv_s.at[h, 1], kv_r.at[h, 1], at_x(-1))
        for k in (2, 1):
            q_copies[h, k] = remote(query, qs.at[h, k], q_s.at[h, k - 1], q_r.at[h, k - 1], at_z(others[k]))
        q_copies[h, 2].start()
        kv_copies[h, 1].start()
        kv_copies[h, 3].start()
        q_copies[h, 1].start()
    for h in range(HEADS):
        kv_copies[h, 1].wait_recv()
        kv_copies[h, "k"] = remote(kv.at[h, 1, 0], kv.at[h, 2, 0], kv_s.at[h, 2], kv_r.at[h, 2], at_x(1))
        kv_copies[h, "k"].start()
        kv_copies[h, 3].wait_recv()
        kv_copies[h, "v"] = remote(kv.at[h, 3, 1], kv.at[h, 2, 1], kv_s.at[h, 3], kv_r.at[h, 3], at_x(-1))
        kv_copies[h, "v"].start()
        q_copies[h, 2].wait_recv()
        q_copies[h, 3] = remote(qs.at[h, 2], qs.at[h, 3], q_s.at[h, 2], q_r.at[h, 2], at_z(others[1]))
        q_copies[h, 3].start()

    w_copy = remote(w_ref.at[:, other_side], w_v.at[pl.ds(COLS, COLS)], w_s, w_r, sibling)
    w_copy.start()
    for copy in local:
        copy.wait()

    stat_out[...] = jnp.zeros_like(stat_out)
    o_copies = {}
    for h in range(HEADS):
        cols = slice(h * HD, (h + 1) * HD)
        kv_copies[h, "k"].wait_recv()
        kv_copies[h, "v"].wait_recv()
        q_copies[h, 1].wait_recv()
        q_copies[h, 3].wait_recv()
        keys, values = [], []
        for k in range(RING):
            fresh = stale_v[k, :, :, cols] + kv[h, k].astype(F32)
            keys.append(fresh[0].astype(BF16))
            values.append(fresh[1].T.astype(BF16))
        keys = jnp.concatenate(keys, axis=0)
        values = jnp.concatenate(values, axis=1)
        for k in (2, 1, 3, 0):
            scores = lax.dot_general(keys, qs[h, k], (((1,), (1,)), ((), ())), preferred_element_type=F32)
            peak = jnp.max(scores, axis=0, keepdims=True)
            expo = jnp.exp((scores - peak) * SCALE)
            denom = jnp.sum(expo, axis=0, keepdims=True)
            mixed = jnp.dot(values, expo.astype(BF16), preferred_element_type=F32) / denom
            buffer = part_out if k else part_in
            buffer[h, k] = mixed.astype(BF16)
            stat_out[k, h : h + 1, :] = peak * SCALE + jnp.log(denom)
        for k in (2, 3, 1):
            o_copies[h, k] = remote(
                part_out.at[h, k], part_in.at[h, k], o_s.at[h, k - 1], o_r.at[h, k - 1], at_z(others[k])
            )
            o_copies[h, k].start()
            if h == HEADS - 1:
                o_copies["t", k] = remote(
                    stat_out.at[k], stat_in.at[k], t_s.at[k - 1], t_r.at[k - 1], at_z(others[k])
                )
                o_copies["t", k].start()

    logs = [stat_out[0]]
    for k in (1, 2, 3):
        o_copies["t", k].wait_recv()
        logs.append(stat_in[k])
    top = functools.reduce(jnp.maximum, logs)
    shares = [jnp.exp(log - top) for log in logs]
    total = functools.reduce(jnp.add, shares)
    shares = [share / total for share in shares]
    a_copies = {}
    for h in range(HEADS):
        terms = []
        for k in range(RING):
            if k:
                o_copies[h, k].wait_recv()
            terms.append(part_in[h, k].astype(F32) * shares[k][h : h + 1])
        merged = functools.reduce(jnp.add, terms).T
        merged = jnp.concatenate(
            [merged[(zz * 8 + yy * 2 + c) * 8 :][:8] for yy in range(RING) for zz in range(2) for c in range(2)], axis=0
        )
        att[:, h * HD : (h + 1) * HD] = merged.astype(BF16)
        a_copies[h] = remote(
            att.at[:, pl.ds(h * HD, HD)], att.at[:, pl.ds(COLS + h * HD, HD)], a_s.at[h], a_r.at[h], sibling
        )
        a_copies[h].start()

    weight.wait()
    w_copy.wait_recv()
    for h in range(HEADS):
        a_copies[h].wait_recv()
    y_copies, z_copies = {}, {}

    def project(j):
        cols = slice(j * WIDTH, (j + 1) * WIDTH)
        pair = jnp.dot(att[...], w_v[:, cols], preferred_element_type=F32).reshape(RING, 32, WIDTH)
        own[:, :, cols] = pair
        for i in range(2):
            y_out[j, i] = pair[:, :, i * HALF : (i + 1) * HALF].astype(BF16)
        far = lax.rem(y + 2, RING)
        for i, step in enumerate((1, -1)):
            y_copies[j, i] = remote(
                y_out.at[j, i, far], y_in.at[j, i], y_s.at[j, i], y_r.at[j, i], at_y(step)
            )
            y_copies[j, i].start()

    def direct_y(j):
        for i, step in enumerate((1, -1)):
            y_copies[j, 2 + i] = remote(
                y_out.at[j, 1 - i, lax.rem(y + step + RING, RING)],
                y_in.at[j, 2 + i], y_s.at[j, 2 + i], y_r.at[j, 2 + i], at_y(step),
            )
            y_copies[j, 2 + i].start()

    def relay_y(j):
        for i, step in enumerate((1, -1)):
            place = lax.rem(y + step + RING, RING)
            y_copies[j, i].wait_recv()
            start = j * WIDTH + i * HALF
            total = own[place, :, start : start + HALF] + y_in[j, i].astype(F32)
            y_sum[j, i] = total.astype(BF16)
            y_copies[j, 4 + i] = remote(
                y_sum.at[j, i], y_in.at[j, 4 + i], y_s.at[j, 4 + i], y_r.at[j, 4 + i], at_y(step)
            )
            y_copies[j, 4 + i].start()

    def to_z(j):
        for i in range(2):
            y_copies[j, 4 + i].wait_recv()
            y_copies[j, 3 - i].wait_recv()
            start = j * WIDTH + i * HALF
            total = own[y, :, start : start + HALF] + y_in[j, 4 + i].astype(F32) + y_in[j, 3 - i].astype(F32)
            z_own[:, :, :, start : start + HALF] = total.reshape(2, 2, 8, HALF)
        for i, (place, owner, device) in enumerate(
            ((z_hi, 1 - core, sibling), (1 - z_hi, core, across), (1 - z_hi, 1 - core, opposite))
        ):
            away = z_own[place, owner, :, j * WIDTH : (j + 1) * WIDTH]
            z_out[j, i] = jnp.concatenate([away[:, :HALF], away[:, HALF:]], axis=0).astype(BF16)
            z_copies[j, i] = remote(z_out.at[j, i], z_in.at[j, i], z_s.at[j, i], z_r.at[j, i], device)
            z_copies[j, i].start()

    def finish(j):
        for i in range(3):
            z_copies[j, i].wait_recv()
        here, there = z_in[j, 1].astype(F32), z_in[j, 0].astype(F32) + z_in[j, 2].astype(F32)
        for i in range(2):
            start = j * WIDTH + i * HALF
            rows = slice(i * 8, (i + 1) * 8)
            mine = z_own[z_hi, core, :, start : start + HALF] + here[rows]
            out_ref[:, pl.ds(pl.multiple_of(core * SIDE + start, HD), HALF)] = mine.astype(BF16)
            out_ref[:, pl.ds(pl.multiple_of((1 - core) * SIDE + start, HD), HALF)] = there[rows].astype(BF16)

    stages = (project, direct_y, relay_y, to_z, finish)
    lags = (0, 3, 4, 7, 11)
    for t in range(CHUNKS + lags[-1]):
        for stage, lag in zip(stages, lags):
            if 0 <= t - lag < CHUNKS:
                stage(t - lag)

    for copies in (kv_copies, q_copies, o_copies, a_copies, y_copies, z_copies):
        for copy in copies.values():
            copy.wait_send()
    w_copy.wait_send()


def body(queries, stale_kv, delta_kv, out_weight):
    dma = pltpu.SemaphoreType.DMA
    return pl.pallas_call(
        kernel,
        name="sublayer",
        out_shape=pltpu.VMEM((8, D), BF16),
        in_specs=[pl.BlockSpec(memory_space=pl.ANY)] * 4,
        out_specs=pl.BlockSpec(memory_space=pltpu.VMEM),
        scratch_shapes=[
            pltpu.VMEM((RING, 2, TOK, COLS), F32),
            pltpu.VMEM((HEADS, RING, 2, TOK, HD), BF16),
            pltpu.VMEM((HEADS, RING, TOK, HD), BF16),
            pltpu.VMEM((HEADS, RING, HD, TOK), BF16),
            pltpu.VMEM((HEADS, RING, HD, TOK), BF16),
            pltpu.VMEM((RING, 8, TOK), F32),
            pltpu.VMEM((RING, 8, TOK), F32),
            pltpu.VMEM((2 * COLS, SIDE), BF16),
            pltpu.VMEM((TOK, 2 * COLS), BF16),
            pltpu.VMEM((RING, 32, SIDE), F32),
            pltpu.VMEM((CHUNKS, 2, RING, 32, HALF), BF16),
            pltpu.VMEM((CHUNKS, 6, 32, HALF), BF16),
            pltpu.VMEM((CHUNKS, 2, 32, HALF), BF16),
            pltpu.VMEM((2, 2, 8, SIDE), F32),
            pltpu.VMEM((CHUNKS, 3, 16, HALF), BF16),
            pltpu.VMEM((CHUNKS, 3, 16, HALF), BF16),
            dma((11,)),
            dma((HEADS, 4)),
            dma((HEADS, 4)),
            dma((HEADS, 3)),
            dma((HEADS, 3)),
            dma((HEADS, 3)),
            dma((HEADS, 3)),
            dma((3,)),
            dma((3,)),
            dma,
            dma,
            dma((HEADS,)),
            dma((HEADS,)),
            dma((CHUNKS, 6)),
            dma((CHUNKS, 6)),
            dma((CHUNKS, 3)),
            dma((CHUNKS, 3)),
        ],
        compiler_params=pltpu.CompilerParams(
            collective_id=0, has_side_effects=True, vmem_limit_bytes=60 * 1024 * 1024
        ),
    )(*[pltpu.with_memory_space_constraint(a, pltpu.HBM) for a in (queries, stale_kv, delta_kv, out_weight)])


def solution(mesh):
    return jax.shard_map(
        body,
        mesh=mesh,
        in_specs=(
            P("patch", "head"),
            P(None, None, "head"),
            P(None, "patch", "head"),
            P("head", None),
        ),
        out_specs=P(("patch", "head"), None),
        check_vma=False,
    )
```

```python
import functools
import math

import jax
import jax.numpy as jnp
from jax import lax
from jax.experimental import pallas as pl
from jax.experimental.pallas import tpu as pltpu
from jax.sharding import PartitionSpec as P

MESH = pl.DeviceIdType.MESH
F32, BF16 = jnp.float32, jnp.bfloat16

HD = 128
HEADS = 3
TOK = 128
RING = 4
COLS = HEADS * HD
D = 6144
CHUNKS = 4
SIDE = D // 2
WIDTH = SIDE // CHUNKS
HALF = WIDTH // 2
SCALE = 1.0 / math.sqrt(HD)


def kernel(
    q_ref, stale_ref, delta_ref, w_ref, out_ref,
    stale_v, kv, qs, part_out, part_in, stat_out, stat_in, w_v, att, own, y_out, y_in, y_sum, z_own, z_out, z_in,
    local_sem, kv_s, kv_r, q_s, q_r, o_s, o_r, t_s, t_r, w_s, w_r, a_s, a_r, y_s, y_r, z_s, z_r,
):
    patch, head = lax.axis_index("patch"), lax.axis_index("head")
    z, x = patch // RING, lax.rem(patch, RING)
    z_hi, y, core = head // 8, lax.rem(head // 2, RING), lax.rem(head, 2)

    def at_x(k):
        return (z * RING + lax.rem(x + k + RING, RING), head)

    def at_z(place):
        return (place * RING + x, head)

    def at_y(k):
        return (patch, z_hi * 8 + lax.rem(y + k + RING, RING) * 2 + core)

    others = {1: z + 1 - 2 * lax.rem(z, 2), 2: lax.rem(z + 2, RING), 3: 3 - z}
    sibling = (patch, z_hi * 8 + y * 2 + (1 - core))
    across = (patch, (1 - z_hi) * 8 + y * 2 + core)
    opposite = (patch, (1 - z_hi) * 8 + y * 2 + (1 - core))

    def remote(src, dst, send, recv, device):
        return pltpu.make_async_remote_copy(
            src_ref=src, dst_ref=dst, send_sem=send, recv_sem=recv, device_id=device, device_id_type=MESH
        )

    local = []
    for k in range(RING):
        row = (z * RING + lax.rem(x - k + RING, RING)) * TOK
        local.append(pltpu.make_async_copy(stale_ref.at[:, pl.ds(row, TOK), :], stale_v.at[k], local_sem.at[k]))
    for h in range(HEADS):
        cols = pl.ds(h * HD, HD)
        local.append(pltpu.make_async_copy(delta_ref.at[:, :, cols], kv.at[h, 0], local_sem.at[4 + h]))
        local.append(pltpu.make_async_copy(q_ref.at[:, cols], qs.at[h, 0], local_sem.at[7 + h]))
    side = pl.ds(pl.multiple_of(core * SIDE, SIDE), SIDE)
    other_side = pl.ds(pl.multiple_of((1 - core) * SIDE, SIDE), SIDE)
    weight = pltpu.make_async_copy(w_ref.at[:, side], w_v.at[pl.ds(0, COLS)], local_sem.at[10])
    for copy in local:
        copy.start()
    weight.start()

    barrier = pltpu.get_barrier_semaphore()
    partners = [at_x(1), at_x(-1), at_y(1), at_y(-1)] + [at_z(others[k]) for k in (1, 2, 3)] + [sibling, across, opposite]
    for device in partners:
        pl.semaphore_signal(barrier, inc=1, device_id=device, device_id_type=MESH)
    pl.semaphore_wait(barrier, len(partners))

    kv_copies, q_copies = {}, {}
    for h in range(HEADS):
        cols = pl.ds(h * HD, HD)
        mine, query = delta_ref.at[:, :, cols], q_ref.at[:, cols]
        kv_copies[h, 1] = remote(mine, kv.at[h, 1], kv_s.at[h, 0], kv_r.at[h, 0], at_x(1))
        kv_copies[h, 3] = remote(mine, kv.at[h, 3], kv_s.at[h, 1], kv_r.at[h, 1], at_x(-1))
        for k in (2, 1):
            q_copies[h, k] = remote(query, qs.at[h, k], q_s.at[h, k - 1], q_r.at[h, k - 1], at_z(others[k]))
        q_copies[h, 2].start()
        kv_copies[h, 1].start()
        kv_copies[h, 3].start()
        q_copies[h, 1].start()
    for h in range(HEADS):
        kv_copies[h, 1].wait_recv()
        kv_copies[h, "k"] = remote(kv.at[h, 1, 0], kv.at[h, 2, 0], kv_s.at[h, 2], kv_r.at[h, 2], at_x(1))
        kv_copies[h, "k"].start()
        kv_copies[h, 3].wait_recv()
        kv_copies[h, "v"] = remote(kv.at[h, 3, 1], kv.at[h, 2, 1], kv_s.at[h, 3], kv_r.at[h, 3], at_x(-1))
        kv_copies[h, "v"].start()
        q_copies[h, 2].wait_recv()
        q_copies[h, 3] = remote(qs.at[h, 2], qs.at[h, 3], q_s.at[h, 2], q_r.at[h, 2], at_z(others[1]))
        q_copies[h, 3].start()

    w_copy = remote(w_ref.at[:, other_side], w_v.at[pl.ds(COLS, COLS)], w_s, w_r, sibling)
    w_copy.start()
    for copy in local:
        copy.wait()

    stat_out[...] = jnp.zeros_like(stat_out)
    o_copies = {}
    for h in range(HEADS):
        cols = slice(h * HD, (h + 1) * HD)
        kv_copies[h, "k"].wait_recv()
        kv_copies[h, "v"].wait_recv()
        q_copies[h, 1].wait_recv()
        q_copies[h, 3].wait_recv()
        keys, values = [], []
        for k in range(RING):
            fresh = stale_v[k, :, :, cols] + kv[h, k].astype(F32)
            keys.append(fresh[0].astype(BF16))
            values.append(fresh[1].T.astype(BF16))
        keys = jnp.concatenate(keys, axis=0)
        values = jnp.concatenate(values, axis=1)
        def block(k):
            scores = lax.dot_general(keys, qs[h, k], (((1,), (1,)), ((), ())), preferred_element_type=F32)
            peak = jnp.max(scores, axis=0, keepdims=True)
            expo = jnp.exp((scores - peak) * SCALE)
            denom = jnp.sum(expo, axis=0, keepdims=True)
            mixed = jnp.dot(values, expo.astype(BF16), preferred_element_type=F32) / denom
            buffer = part_out if k else part_in
            buffer[h, k] = mixed.astype(BF16)
            stat_out[k, h : h + 1, :] = peak * SCALE + jnp.log(denom)

        for k in (2, 1, 3):
            block(k)
        for k in (2, 3, 1):
            o_copies[h, k] = remote(
                part_out.at[h, k], part_in.at[h, k], o_s.at[h, k - 1], o_r.at[h, k - 1], at_z(others[k])
            )
            o_copies[h, k].start()
            if h == HEADS - 1:
                o_copies["t", k] = remote(
                    stat_out.at[k], stat_in.at[k], t_s.at[k - 1], t_r.at[k - 1], at_z(others[k])
                )
                o_copies["t", k].start()
        block(0)

    logs = [stat_out[0]]
    for k in (1, 2, 3):
        o_copies["t", k].wait_recv()
        logs.append(stat_in[k])
    top = functools.reduce(jnp.maximum, logs)
    shares = [jnp.exp(log - top) for log in logs]
    total = functools.reduce(jnp.add, shares)
    shares = [share / total for share in shares]
    a_copies = {}
    for h in range(HEADS):
        terms = []
        for k in range(RING):
            if k:
                o_copies[h, k].wait_recv()
            terms.append(part_in[h, k].astype(F32) * shares[k][h : h + 1])
        merged = functools.reduce(jnp.add, terms).T
        merged = jnp.concatenate(
            [merged[(zz * 8 + yy * 2 + c) * 8 :][:8] for yy in range(RING) for zz in range(2) for c in range(2)], axis=0
        )
        att[:, h * HD : (h + 1) * HD] = merged.astype(BF16)
        a_copies[h] = remote(
            att.at[:, pl.ds(h * HD, HD)], att.at[:, pl.ds(COLS + h * HD, HD)], a_s.at[h], a_r.at[h], sibling
        )
        a_copies[h].start()

    weight.wait()
    w_copy.wait_recv()
    for h in range(HEADS):
        a_copies[h].wait_recv()
    y_copies, z_copies = {}, {}

    def project(j):
        cols = slice(j * WIDTH, (j + 1) * WIDTH)
        pair = jnp.dot(att[...], w_v[:, cols], preferred_element_type=F32).reshape(RING, 32, WIDTH)
        own[:, :, cols] = pair
        for i in range(2):
            y_out[j, i] = pair[:, :, i * HALF : (i + 1) * HALF].astype(BF16)
        far = lax.rem(y + 2, RING)
        for i, step in enumerate((1, -1)):
            y_copies[j, i] = remote(
                y_out.at[j, i, far], y_in.at[j, i], y_s.at[j, i], y_r.at[j, i], at_y(step)
            )
            y_copies[j, i].start()

    def direct_y(j):
        for i, step in enumerate((1, -1)):
            y_copies[j, 2 + i] = remote(
                y_out.at[j, 1 - i, lax.rem(y + step + RING, RING)],
                y_in.at[j, 2 + i], y_s.at[j, 2 + i], y_r.at[j, 2 + i], at_y(step),
            )
            y_copies[j, 2 + i].start()

    def relay_y(j):
        for i, step in enumerate((1, -1)):
            place = lax.rem(y + step + RING, RING)
            y_copies[j, i].wait_recv()
            start = j * WIDTH + i * HALF
            total = own[place, :, start : start + HALF] + y_in[j, i].astype(F32)
            y_sum[j, i] = total.astype(BF16)
            y_copies[j, 4 + i] = remote(
                y_sum.at[j, i], y_in.at[j, 4 + i], y_s.at[j, 4 + i], y_r.at[j, 4 + i], at_y(step)
            )
            y_copies[j, 4 + i].start()

    def to_z(j):
        for i in range(2):
            y_copies[j, 4 + i].wait_recv()
            y_copies[j, 3 - i].wait_recv()
            start = j * WIDTH + i * HALF
            total = own[y, :, start : start + HALF] + y_in[j, 4 + i].astype(F32) + y_in[j, 3 - i].astype(F32)
            z_own[:, :, :, start : start + HALF] = total.reshape(2, 2, 8, HALF)
        for i, (place, owner, device) in enumerate(
            ((z_hi, 1 - core, sibling), (1 - z_hi, core, across), (1 - z_hi, 1 - core, opposite))
        ):
            away = z_own[place, owner, :, j * WIDTH : (j + 1) * WIDTH]
            z_out[j, i] = jnp.concatenate([away[:, :HALF], away[:, HALF:]], axis=0).astype(BF16)
            z_copies[j, i] = remote(z_out.at[j, i], z_in.at[j, i], z_s.at[j, i], z_r.at[j, i], device)
            z_copies[j, i].start()

    def finish(j):
        for i in range(3):
            z_copies[j, i].wait_recv()
        here, there = z_in[j, 1].astype(F32), z_in[j, 0].astype(F32) + z_in[j, 2].astype(F32)
        for i in range(2):
            start = j * WIDTH + i * HALF
            rows = slice(i * 8, (i + 1) * 8)
            mine = z_own[z_hi, core, :, start : start + HALF] + here[rows]
            out_ref[:, pl.ds(pl.multiple_of(core * SIDE + start, HD), HALF)] = mine.astype(BF16)
            out_ref[:, pl.ds(pl.multiple_of((1 - core) * SIDE + start, HD), HALF)] = there[rows].astype(BF16)

    stages = (project, direct_y, relay_y, to_z, finish)
    lags = (0, 3, 4, 7, 11)
    for t in range(CHUNKS + lags[-1]):
        for stage, lag in zip(stages, lags):
            if 0 <= t - lag < CHUNKS:
                stage(t - lag)

    for copies in (kv_copies, q_copies, o_copies, a_copies, y_copies, z_copies):
        for copy in copies.values():
            copy.wait_send()
    w_copy.wait_send()


def body(queries, stale_kv, delta_kv, out_weight):
    dma = pltpu.SemaphoreType.DMA
    return pl.pallas_call(
        kernel,
        name="sublayer",
        out_shape=pltpu.VMEM((8, D), BF16),
        in_specs=[pl.BlockSpec(memory_space=pl.ANY)] * 4,
        out_specs=pl.BlockSpec(memory_space=pltpu.VMEM),
        scratch_shapes=[
            pltpu.VMEM((RING, 2, TOK, COLS), F32),
            pltpu.VMEM((HEADS, RING, 2, TOK, HD), BF16),
            pltpu.VMEM((HEADS, RING, TOK, HD), BF16),
            pltpu.VMEM((HEADS, RING, HD, TOK), BF16),
            pltpu.VMEM((HEADS, RING, HD, TOK), BF16),
            pltpu.VMEM((RING, 8, TOK), F32),
            pltpu.VMEM((RING, 8, TOK), F32),
            pltpu.VMEM((2 * COLS, SIDE), BF16),
            pltpu.VMEM((TOK, 2 * COLS), BF16),
            pltpu.VMEM((RING, 32, SIDE), F32),
            pltpu.VMEM((CHUNKS, 2, RING, 32, HALF), BF16),
            pltpu.VMEM((CHUNKS, 6, 32, HALF), BF16),
            pltpu.VMEM((CHUNKS, 2, 32, HALF), BF16),
            pltpu.VMEM((2, 2, 8, SIDE), F32),
            pltpu.VMEM((CHUNKS, 3, 16, HALF), BF16),
            pltpu.VMEM((CHUNKS, 3, 16, HALF), BF16),
            dma((11,)),
            dma((HEADS, 4)),
            dma((HEADS, 4)),
            dma((HEADS, 3)),
            dma((HEADS, 3)),
            dma((HEADS, 3)),
            dma((HEADS, 3)),
            dma((3,)),
            dma((3,)),
            dma,
            dma,
            dma((HEADS,)),
            dma((HEADS,)),
            dma((CHUNKS, 6)),
            dma((CHUNKS, 6)),
            dma((CHUNKS, 3)),
            dma((CHUNKS, 3)),
        ],
        compiler_params=pltpu.CompilerParams(
            collective_id=0, has_side_effects=True, vmem_limit_bytes=60 * 1024 * 1024
        ),
    )(*[pltpu.with_memory_space_constraint(a, pltpu.HBM) for a in (queries, stale_kv, delta_kv, out_weight)])


def solution(mesh):
    return jax.shard_map(
        body,
        mesh=mesh,
        in_specs=(
            P("patch", "head"),
            P(None, None, "head"),
            P(None, "patch", "head"),
            P("head", None),
        ),
        out_specs=P(("patch", "head"), None),
        check_vma=False,
    )
```

```python
import functools
import math

import jax
import jax.numpy as jnp
from jax import lax
from jax.experimental import pallas as pl
from jax.experimental.pallas import tpu as pltpu
from jax.sharding import PartitionSpec as P

MESH = pl.DeviceIdType.MESH
F32, BF16 = jnp.float32, jnp.bfloat16

HD = 128
HEADS = 3
TOK = 128
RING = 4
COLS = HEADS * HD
D = 6144
CHUNKS = 4
SIDE = D // 2
WIDTH = SIDE // CHUNKS
HALF = WIDTH // 2
SCALE = 1.0 / math.sqrt(HD)


def kernel(
    q_ref, stale_ref, delta_ref, w_ref, out_ref,
    stale_v, kv, qs, part_out, part_in, stat_out, stat_in, w_v, att, own, y_out, y_in, y_sum, z_own, z_out, z_in,
    local_sem, kv_s, kv_r, q_s, q_r, o_s, o_r, t_s, t_r, w_s, w_r, a_s, a_r, y_s, y_r, z_s, z_r,
):
    patch, head = lax.axis_index("patch"), lax.axis_index("head")
    z, x = patch // RING, lax.rem(patch, RING)
    z_hi, y, core = head // 8, lax.rem(head // 2, RING), lax.rem(head, 2)

    def at_x(k):
        return (z * RING + lax.rem(x + k + RING, RING), head)

    def at_z(place):
        return (place * RING + x, head)

    def at_y(k):
        return (patch, z_hi * 8 + lax.rem(y + k + RING, RING) * 2 + core)

    others = {1: z + 1 - 2 * lax.rem(z, 2), 2: lax.rem(z + 2, RING), 3: 3 - z}
    sibling = (patch, z_hi * 8 + y * 2 + (1 - core))
    across = (patch, (1 - z_hi) * 8 + y * 2 + core)
    opposite = (patch, (1 - z_hi) * 8 + y * 2 + (1 - core))

    def remote(src, dst, send, recv, device):
        return pltpu.make_async_remote_copy(
            src_ref=src, dst_ref=dst, send_sem=send, recv_sem=recv, device_id=device, device_id_type=MESH
        )

    local = []
    for k in range(RING):
        row = (z * RING + lax.rem(x - k + RING, RING)) * TOK
        local.append(pltpu.make_async_copy(stale_ref.at[:, pl.ds(row, TOK), :], stale_v.at[k], local_sem.at[k]))
    for h in range(HEADS):
        cols = pl.ds(h * HD, HD)
        local.append(pltpu.make_async_copy(delta_ref.at[:, :, cols], kv.at[h, 0], local_sem.at[4 + h]))
        local.append(pltpu.make_async_copy(q_ref.at[:, cols], qs.at[h, 0], local_sem.at[7 + h]))
    side = pl.ds(pl.multiple_of(core * SIDE, SIDE), SIDE)
    other_side = pl.ds(pl.multiple_of((1 - core) * SIDE, SIDE), SIDE)
    weight = pltpu.make_async_copy(w_ref.at[:, side], w_v.at[pl.ds(0, COLS)], local_sem.at[10])

    barrier = pltpu.get_barrier_semaphore()
    partners = [at_x(1), at_x(-1), at_y(1), at_y(-1)] + [at_z(others[k]) for k in (1, 2, 3)] + [sibling, across, opposite]
    for device in partners:
        pl.semaphore_signal(barrier, inc=1, device_id=device, device_id_type=MESH)
    pl.semaphore_wait(barrier, len(partners))

    kv_copies, q_copies = {}, {}
    def send_own(h):
        cols = pl.ds(h * HD, HD)
        mine, query = delta_ref.at[:, :, cols], q_ref.at[:, cols]
        kv_copies[h, 1] = remote(mine, kv.at[h, 1], kv_s.at[h, 0], kv_r.at[h, 0], at_x(1))
        kv_copies[h, 3] = remote(mine, kv.at[h, 3], kv_s.at[h, 1], kv_r.at[h, 1], at_x(-1))
        for k in (2, 1):
            q_copies[h, k] = remote(query, qs.at[h, k], q_s.at[h, k - 1], q_r.at[h, k - 1], at_z(others[k]))
        q_copies[h, 2].start()
        kv_copies[h, 1].start()
        kv_copies[h, 3].start()
        q_copies[h, 1].start()
    def send_relays(h):
        kv_copies[h, 1].wait_recv()
        kv_copies[h, "k"] = remote(kv.at[h, 1, 0], kv.at[h, 2, 0], kv_s.at[h, 2], kv_r.at[h, 2], at_x(1))
        kv_copies[h, "k"].start()
        kv_copies[h, 3].wait_recv()
        kv_copies[h, "v"] = remote(kv.at[h, 3, 1], kv.at[h, 2, 1], kv_s.at[h, 3], kv_r.at[h, 3], at_x(-1))
        kv_copies[h, "v"].start()
        q_copies[h, 2].wait_recv()
        q_copies[h, 3] = remote(qs.at[h, 2], qs.at[h, 3], q_s.at[h, 2], q_r.at[h, 2], at_z(others[1]))
        q_copies[h, 3].start()

    send_own(0)
    send_own(1)
    for copy in local:
        copy.start()
    send_relays(0)
    send_own(2)
    send_relays(1)
    send_relays(2)
    w_copy = remote(w_ref.at[:, other_side], w_v.at[pl.ds(COLS, COLS)], w_s, w_r, sibling)
    w_copy.start()
    weight.start()
    for copy in local:
        copy.wait()

    stat_out[...] = jnp.zeros_like(stat_out)
    o_copies = {}
    for h in range(HEADS):
        cols = slice(h * HD, (h + 1) * HD)
        kv_copies[h, "k"].wait_recv()
        kv_copies[h, "v"].wait_recv()
        q_copies[h, 1].wait_recv()
        q_copies[h, 3].wait_recv()
        keys, values = [], []
        for k in range(RING):
            fresh = stale_v[k, :, :, cols] + kv[h, k].astype(F32)
            keys.append(fresh[0].astype(BF16))
            values.append(fresh[1].T.astype(BF16))
        keys = jnp.concatenate(keys, axis=0)
        values = jnp.concatenate(values, axis=1)
        for k in (2, 1, 3, 0):
            scores = lax.dot_general(keys, qs[h, k], (((1,), (1,)), ((), ())), preferred_element_type=F32)
            peak = jnp.max(scores, axis=0, keepdims=True)
            expo = jnp.exp((scores - peak) * SCALE)
            denom = jnp.sum(expo, axis=0, keepdims=True)
            mixed = jnp.dot(values, expo.astype(BF16), preferred_element_type=F32) / denom
            buffer = part_out if k else part_in
            buffer[h, k] = mixed.astype(BF16)
            stat_out[k, h : h + 1, :] = peak * SCALE + jnp.log(denom)
        for k in (2, 3, 1):
            o_copies[h, k] = remote(
                part_out.at[h, k], part_in.at[h, k], o_s.at[h, k - 1], o_r.at[h, k - 1], at_z(others[k])
            )
            o_copies[h, k].start()
            if h == HEADS - 1:
                o_copies["t", k] = remote(
                    stat_out.at[k], stat_in.at[k], t_s.at[k - 1], t_r.at[k - 1], at_z(others[k])
                )
                o_copies["t", k].start()

    logs = [stat_out[0]]
    for k in (1, 2, 3):
        o_copies["t", k].wait_recv()
        logs.append(stat_in[k])
    top = functools.reduce(jnp.maximum, logs)
    shares = [jnp.exp(log - top) for log in logs]
    total = functools.reduce(jnp.add, shares)
    shares = [share / total for share in shares]
    a_copies = {}
    for h in range(HEADS):
        terms = []
        for k in range(RING):
            if k:
                o_copies[h, k].wait_recv()
            terms.append(part_in[h, k].astype(F32) * shares[k][h : h + 1])
        merged = functools.reduce(jnp.add, terms).T
        merged = jnp.concatenate(
            [merged[(zz * 8 + yy * 2 + c) * 8 :][:8] for yy in range(RING) for zz in range(2) for c in range(2)], axis=0
        )
        att[:, h * HD : (h + 1) * HD] = merged.astype(BF16)
        a_copies[h] = remote(
            att.at[:, pl.ds(h * HD, HD)], att.at[:, pl.ds(COLS + h * HD, HD)], a_s.at[h], a_r.at[h], sibling
        )
        a_copies[h].start()

    weight.wait()
    w_copy.wait_recv()
    for h in range(HEADS):
        a_copies[h].wait_recv()
    y_copies, z_copies = {}, {}

    def project(j):
        cols = slice(j * WIDTH, (j + 1) * WIDTH)
        pair = jnp.dot(att[...], w_v[:, cols], preferred_element_type=F32).reshape(RING, 32, WIDTH)
        own[:, :, cols] = pair
        for i in range(2):
            y_out[j, i] = pair[:, :, i * HALF : (i + 1) * HALF].astype(BF16)
        far = lax.rem(y + 2, RING)
        for i, step in enumerate((1, -1)):
            y_copies[j, i] = remote(
                y_out.at[j, i, far], y_in.at[j, i], y_s.at[j, i], y_r.at[j, i], at_y(step)
            )
            y_copies[j, i].start()

    def direct_y(j):
        for i, step in enumerate((1, -1)):
            y_copies[j, 2 + i] = remote(
                y_out.at[j, 1 - i, lax.rem(y + step + RING, RING)],
                y_in.at[j, 2 + i], y_s.at[j, 2 + i], y_r.at[j, 2 + i], at_y(step),
            )
            y_copies[j, 2 + i].start()

    def relay_y(j):
        for i, step in enumerate((1, -1)):
            place = lax.rem(y + step + RING, RING)
            y_copies[j, i].wait_recv()
            start = j * WIDTH + i * HALF
            total = own[place, :, start : start + HALF] + y_in[j, i].astype(F32)
            y_sum[j, i] = total.astype(BF16)
            y_copies[j, 4 + i] = remote(
                y_sum.at[j, i], y_in.at[j, 4 + i], y_s.at[j, 4 + i], y_r.at[j, 4 + i], at_y(step)
            )
            y_copies[j, 4 + i].start()

    def to_z(j):
        for i in range(2):
            y_copies[j, 4 + i].wait_recv()
            y_copies[j, 3 - i].wait_recv()
            start = j * WIDTH + i * HALF
            total = own[y, :, start : start + HALF] + y_in[j, 4 + i].astype(F32) + y_in[j, 3 - i].astype(F32)
            z_own[:, :, :, start : start + HALF] = total.reshape(2, 2, 8, HALF)
        for i, (place, owner, device) in enumerate(
            ((z_hi, 1 - core, sibling), (1 - z_hi, core, across), (1 - z_hi, 1 - core, opposite))
        ):
            away = z_own[place, owner, :, j * WIDTH : (j + 1) * WIDTH]
            z_out[j, i] = jnp.concatenate([away[:, :HALF], away[:, HALF:]], axis=0).astype(BF16)
            z_copies[j, i] = remote(z_out.at[j, i], z_in.at[j, i], z_s.at[j, i], z_r.at[j, i], device)
            z_copies[j, i].start()

    def finish(j):
        for i in range(3):
            z_copies[j, i].wait_recv()
        here, there = z_in[j, 1].astype(F32), z_in[j, 0].astype(F32) + z_in[j, 2].astype(F32)
        for i in range(2):
            start = j * WIDTH + i * HALF
            rows = slice(i * 8, (i + 1) * 8)
            mine = z_own[z_hi, core, :, start : start + HALF] + here[rows]
            out_ref[:, pl.ds(pl.multiple_of(core * SIDE + start, HD), HALF)] = mine.astype(BF16)
            out_ref[:, pl.ds(pl.multiple_of((1 - core) * SIDE + start, HD), HALF)] = there[rows].astype(BF16)

    stages = (project, direct_y, relay_y, to_z, finish)
    lags = (0, 3, 4, 8, 12)
    for t in range(CHUNKS + lags[-1]):
        for stage, lag in zip(stages, lags):
            if 0 <= t - lag < CHUNKS:
                stage(t - lag)

    for copies in (kv_copies, q_copies, o_copies, a_copies, y_copies, z_copies):
        for copy in copies.values():
            copy.wait_send()
    w_copy.wait_send()


def body(queries, stale_kv, delta_kv, out_weight):
    dma = pltpu.SemaphoreType.DMA
    return pl.pallas_call(
        kernel,
        name="sublayer",
        out_shape=pltpu.VMEM((8, D), BF16),
        in_specs=[pl.BlockSpec(memory_space=pl.ANY)] * 4,
        out_specs=pl.BlockSpec(memory_space=pltpu.VMEM),
        scratch_shapes=[
            pltpu.VMEM((RING, 2, TOK, COLS), F32),
            pltpu.VMEM((HEADS, RING, 2, TOK, HD), BF16),
            pltpu.VMEM((HEADS, RING, TOK, HD), BF16),
            pltpu.VMEM((HEADS, RING, HD, TOK), BF16),
            pltpu.VMEM((HEADS, RING, HD, TOK), BF16),
            pltpu.VMEM((RING, 8, TOK), F32),
            pltpu.VMEM((RING, 8, TOK), F32),
            pltpu.VMEM((2 * COLS, SIDE), BF16),
            pltpu.VMEM((TOK, 2 * COLS), BF16),
            pltpu.VMEM((RING, 32, SIDE), F32),
            pltpu.VMEM((CHUNKS, 2, RING, 32, HALF), BF16),
            pltpu.VMEM((CHUNKS, 6, 32, HALF), BF16),
            pltpu.VMEM((CHUNKS, 2, 32, HALF), BF16),
            pltpu.VMEM((2, 2, 8, SIDE), F32),
            pltpu.VMEM((CHUNKS, 3, 16, HALF), BF16),
            pltpu.VMEM((CHUNKS, 3, 16, HALF), BF16),
            dma((11,)),
            dma((HEADS, 4)),
            dma((HEADS, 4)),
            dma((HEADS, 3)),
            dma((HEADS, 3)),
            dma((HEADS, 3)),
            dma((HEADS, 3)),
            dma((3,)),
            dma((3,)),
            dma,
            dma,
            dma((HEADS,)),
            dma((HEADS,)),
            dma((CHUNKS, 6)),
            dma((CHUNKS, 6)),
            dma((CHUNKS, 3)),
            dma((CHUNKS, 3)),
        ],
        compiler_params=pltpu.CompilerParams(
            collective_id=0, has_side_effects=True, vmem_limit_bytes=60 * 1024 * 1024
        ),
    )(*[pltpu.with_memory_space_constraint(a, pltpu.HBM) for a in (queries, stale_kv, delta_kv, out_weight)])


def solution(mesh):
    return jax.shard_map(
        body,
        mesh=mesh,
        in_specs=(
            P("patch", "head"),
            P(None, None, "head"),
            P(None, "patch", "head"),
            P("head", None),
        ),
        out_specs=P(("patch", "head"), None),
        check_vma=False,
    )
```
